128 devices in a mesh: replica: 8 (over y_hi, z), tp: 16 (over x, y_lo, core).
Axes of the slice: x: 4, y: 4 (y_hi: 2, y_lo: 2; y = y_hi * 2 + y_lo), z: 4, core: 2. Of those that a mesh axis runs over, the one named last changes fastest.
Arguments:
- changed_layers: int32 [4], replicated, may hold values from 0 to 3, each once
- bucket_owner: int32 [16], replicated, may hold values from 0 to 15, each once
- query_up: bfloat16 [4, 1536, 16384], P(None, ('replica', 'tp')), may hold values from -0.5 to 0.5
- key_up: bfloat16 [4, 512, 16384], P(None, ('replica', 'tp')), may hold values from -0.5 to 0.5
- query_latent: bfloat16 [6144, 1536], P('replica'), may hold values from -1.796875 to 1.796875
Outputs:
- absorbed: bfloat16 [1, 128, 1536, 512], P(None, 'tp')
- query_absorbed: bfloat16 [1, 6144, 128, 512], P(None, 'replica', 'tp')
The draws below stay inside these ranges and needn't reach their ends.
Inputs may be any that keep to these rules, and one draw needn't show every extreme that they name: `changed_layers`: distinct held layers. `bucket_owner`: each tp position owns exactly one bucket.
All inputs are finite; a program needn't handle non-finite values.
Results may differ from the reference program's by a relative error of at most 0.0049.
Values may be sent and summed in bfloat16 or wider, within the bound.
A program may use at most 128 MiB of HBM per device.

```python
import jax
import jax.numpy as jnp
from jax import lax

HEADS = 128
Q_LATENT = 1536
KV_LATENT = 512
HEAD_NOPE = 128
HELD_LAYERS = 4
REFRESHED = 1
BUCKETS = 16
ALL_QUEUED = 6144
N_REPLICA = 8


def shard_levels(rng, shape, shards, least, largest):
    level = 1.0
    for axis_at, shards_of in shards:
        steps = jax.random.uniform(jax.random.fold_in(jax.random.fold_in(rng, 6), axis_at), (shards_of,), jnp.float32, least / len(shards), largest / len(shards))
        level = level * jnp.repeat(jnp.exp(steps), shape[axis_at] // shards_of).reshape((-1,) + (1,) * (len(shape) - 1 - axis_at))
    return level


def gaussian(rng, shape, width, limit, pieces=(), held_as=jnp.bfloat16):
    result = jax.random.normal(rng, shape, jnp.float32) * width
    if len(pieces) > 0:
        result = shard_levels(rng, shape, pieces, -0.22, 0.18) * result
    return jnp.clip(result, min=-limit, max=limit).astype(held_as)


def setup_inputs(seed: int = 0) -> dict:
    keys = jax.random.split(jax.random.key(seed), 6)
    changed_layers = jax.random.permutation(keys[0], HELD_LAYERS).astype(jnp.int32)
    bucket_owner = jax.random.permutation(keys[1], BUCKETS).astype(jnp.int32)
    query_up = gaussian(keys[2], (HELD_LAYERS, Q_LATENT, HEADS * HEAD_NOPE), HEAD_NOPE ** -0.5, 0.5, ((1, 128),))
    key_up = gaussian(keys[3], (HELD_LAYERS, KV_LATENT, HEADS * HEAD_NOPE), HEAD_NOPE ** -0.5, 0.5, ((1, 128),))
    query_latent = gaussian(keys[4], (ALL_QUEUED, Q_LATENT), 0.3, 1.796875, ((0, 8),))
    return {"changed_layers": changed_layers, "bucket_owner": bucket_owner, "query_up": query_up, "key_up": key_up, "query_latent": query_latent}


def regroup_rows(weight, bucket_owner):
    rows, cols = weight.shape
    blocks = weight.reshape(N_REPLICA, BUCKETS, rows // (N_REPLICA * BUCKETS), cols)
    return jnp.take(blocks, bucket_owner, axis=1).reshape(rows, cols)


def reference(changed_layers, bucket_owner, query_up, key_up, query_latent):
    absorbed_all = []
    queries_all = []
    for window_slot in range(REFRESHED):
        layer_id = changed_layers[window_slot].astype(jnp.int32)
        up_query = regroup_rows(lax.dynamic_index_in_dim(query_up, layer_id, 0, keepdims=False), bucket_owner)
        up_key = regroup_rows(lax.dynamic_index_in_dim(key_up, layer_id, 0, keepdims=False), bucket_owner)
        query_heads = up_query.reshape(Q_LATENT, HEADS, HEAD_NOPE).transpose(1, 0, 2)
        key_heads = up_key.reshape(KV_LATENT, HEADS, HEAD_NOPE).transpose(1, 0, 2)

        def one_head(pair):
            matrix = lax.dot_general(pair[0], pair[1], (((1,), (1,)), ((), ())),
                                     preferred_element_type=jnp.float32).astype(jnp.bfloat16)
            projected = jnp.dot(query_latent, matrix, preferred_element_type=jnp.float32).astype(jnp.bfloat16)
            return matrix, projected

        matrices, projected = lax.map(one_head, (query_heads, key_heads))
        absorbed_all.append(matrices)
        queries_all.append(projected.transpose(1, 0, 2))
    return jnp.stack(absorbed_all), jnp.stack(queries_all)
```

```python
import jax
import jax.numpy as jnp
from jax import lax
from jax.experimental import pallas as pl
from jax.experimental.pallas import tpu as pltpu
from jax.sharding import PartitionSpec as P

MESH = pl.DeviceIdType.MESH
BF16, F32 = jnp.bfloat16, jnp.float32

DX = (0, 1, 3, 2)
EF = ((0, 0), (0, 1), (1, 0), (1, 1))
NEAR = [(dx, e, f) for dx in DX for e, f in EF]
QROWS, KROWS, ROWS = 12, 4, 16
COLS = 1024
LAYERS = 4


def place():
    r, t = lax.axis_index("replica"), lax.axis_index("tp")
    return t // 4, (t // 2) % 2, t % 2, r // 4, r % 4


def flip(bit, by):
    return 1 - bit if by else bit


def relative(dx, e, f, g, dz):
    x, y_lo, c, y_hi, z = place()
    return flip(y_hi, g) * 4 + (z + dz) % 4, (((x + dx) % 4) * 2 + flip(y_lo, e)) * 2 + flip(c, f)


def back(rel):
    return ((4 - rel[0]) % 4,) + tuple(rel[1:])


def number(rel, g):
    return (rel[0] * 4 + rel[1] * 2 + rel[2]) * 2 + g


def selections(owner_ref):
    out = lax.broadcasted_iota(jnp.int32, (256, 256), 0)
    raw = lax.broadcasted_iota(jnp.int32, (256, 256), 1)
    wanted = jnp.zeros((256, 256), jnp.int32)
    for b in range(16):
        start = owner_ref[b] * ROWS
        wanted = jnp.where((out >= b * QROWS) & (out < (b + 1) * QROWS), start + out - b * QROWS, wanted)
        key_from = 16 * QROWS + b * KROWS
        wanted = jnp.where((out >= key_from) & (out < key_from + KROWS), start + QROWS + out - key_from, wanted)
    return jnp.where(raw == wanted, 1.0, 0.0).astype(BF16)


def gather_kernel(layer_ref, owner_ref, q_hbm, k_hbm, lat_hbm, uq_ref, uk_ref, p_ref,
                  qv, kv, lat, mine, held, sel, spread, acc, load_sem, send_sem, recv_sem):
    x, y_lo, c, y_hi, z = place()
    me_r, me_t = relative(0, 0, 0, 0, 0)
    barrier = pltpu.get_barrier_semaphore()
    partners = [relative(*rel, g, 0) for rel in NEAR for g in range(2) if any(rel) or g]
    partners += [relative(0, 0, 0, 0, dz) for dz in (1, 3)]
    for to in partners:
        pl.semaphore_signal(barrier, inc=1, device_id=to, device_id_type=MESH)

    loads = []
    for i, dx in enumerate(DX):
        columns = pl.ds(pl.multiple_of(((x + dx) % 4) * 4 * COLS, 4 * COLS), 4 * COLS)
        loads.append(pltpu.make_async_copy(q_hbm.at[:, :, columns], qv.at[i], load_sem.at[i]))
    load_k = pltpu.make_async_copy(k_hbm, kv, load_sem.at[4])
    load_lat = pltpu.make_async_copy(lat_hbm, lat, load_sem.at[5])
    load_k.start()
    for load in loads:
        load.start()
    load_lat.start()

    layer = layer_ref[0]
    row = lax.broadcasted_iota(jnp.int32, (ROWS, LAYERS * ROWS), 0)
    raw = lax.broadcasted_iota(jnp.int32, (ROWS, LAYERS * ROWS), 1)
    pick = jnp.where(row < QROWS, row * LAYERS + layer, LAYERS * QROWS + layer * KROWS + row - QROWS)
    pick = jnp.where(raw == pick, 1.0, 0.0).astype(BF16)

    def pack(i, e, f):
        dx = DX[i]
        _, to_t = relative(dx, e, f, 0, 0)
        inner = (to_t % 4) * COLS
        from_q = qv[i, :, :, pl.ds(pl.multiple_of(inner, COLS), COLS)].reshape(LAYERS * QROWS, COLS)
        from_k = kv[:, :, pl.ds(pl.multiple_of(to_t * COLS, COLS), COLS)].reshape(LAYERS * KROWS, COLS)
        return jnp.dot(pick, jnp.concatenate([from_q, from_k], 0), preferred_element_type=F32).astype(BF16)

    sends = []

    def send(source, to, there, number_there, dz_there):
        copy = pltpu.make_async_remote_copy(
            src_ref=source, dst_ref=held.at[there[0], there[1]], send_sem=send_sem.at[len(sends)],
            recv_sem=recv_sem.at[dz_there, number_there], device_id=to, device_id_type=MESH)
        copy.start()
        sends.append(copy)

    def arrive(rel, g, dz):
        there = relative(*rel, g, dz)
        block = held.at[there[0], there[1]]
        pltpu.make_async_remote_copy(
            src_ref=block, dst_ref=block, send_sem=send_sem.at[0], recv_sem=recv_sem.at[dz, number(rel, g)],
            device_id=partners[0], device_id_type=MESH).wait_recv()
        return there, block

    def along_z(there, block, rel, g, dz, up):
        to = relative(0, 0, 0, 0, 1 if up else 3)
        send(block, to, there, number(rel, g), (dz + (3 if up else 1)) % 4)

    load_k.wait()
    for i in range(4):
        loads[i].wait()
        for e, f in EF:
            rel = (DX[i], e, f)
            block = pack(i, e, f)
            if any(rel):
                mine[i * 4 + e * 2 + f] = block
            else:
                held[me_r, me_t] = block
        if i == 0:
            pl.semaphore_wait(barrier, len(partners))
            own = held.at[me_r, me_t]
            for up in (True, False):
                along_z((me_r, me_t), own, (0, 0, 0), 0, 0, up)
        for e, f in EF:
            rel = (DX[i], e, f)
            if any(rel):
                send(mine.at[i * 4 + e * 2 + f], relative(*rel, 0, 0), (me_r, me_t), number(back(rel), 0), 0)
    for i in range(4):
        for e, f in EF:
            rel = (DX[i], e, f)
            source = mine.at[i * 4 + e * 2 + f] if any(rel) else own
            send(source, relative(*rel, 1, 0), (me_r, me_t), number(back(rel), 1), 0)

    order = [back(rel) for rel in NEAR]
    for rel in order:
        if any(rel):
            there, block = arrive(rel, 0, 0)
            for up in (True, False):
                along_z(there, block, rel, 0, 0, up)
    for rel in order:
        up = rel[2] == 0
        there, block = arrive(rel, 0, 3 if up else 1)
        along_z(there, block, rel, 0, 3 if up else 1, up)
    for rel in order:
        there, block = arrive(rel, 1, 0)
        for up in (True, False):
            along_z(there, block, rel, 1, 0, up)

    sel[...] = selections(owner_ref)
    load_lat.wait()
    pair_q = sel[0:192, :]
    zero = jnp.zeros((192, 256), BF16)
    pair_q = jnp.concatenate([jnp.concatenate([pair_q, zero], 1), jnp.concatenate([zero, pair_q], 1)], 0)
    for pair in range(4):
        both = jnp.dot(lat[:, pair * 384:(pair + 1) * 384], pair_q, preferred_element_type=F32).astype(BF16)
        spread[2 * pair] = both[:, :256]
        spread[2 * pair + 1] = both[:, 256:]

    def absorb_slab(g, dz, first=False, last=False):
        r, _ = relative(0, 0, 0, g, dz)
        slab = held[r].reshape(256, COLS)
        ordered = jnp.dot(sel[...], slab, preferred_element_type=F32).astype(BF16)
        uq_ref[r] = ordered[:192]
        uk_ref[r] = ordered[192:]
        term = jnp.dot(spread[r], slab, preferred_element_type=F32)
        total = term if first else acc[...] + term
        if last:
            p_ref[...] = total.astype(BF16)
        else:
            acc[...] = total

    absorb_slab(0, 0, first=True)
    for rel in order:
        there, block = arrive(rel, 0, 2)
        send(block, relative(0, 0, 0, 1, 0), there, number(rel, 1), 2)
    absorb_slab(1, 0)
    for dz in (1, 3):
        for rel in order:
            if rel[2] == (1 if dz == 3 else 0):
                arrive(rel, 0, dz)
        absorb_slab(0, dz)
    absorb_slab(0, 2)
    for rel in order:
        arrive(rel, 1, 2)
    absorb_slab(1, 2)
    for dz in (1, 3):
        for rel in order:
            arrive(rel, 1, dz)
        absorb_slab(1, dz, last=dz == 3)
    for copy in sends:
        copy.wait_send()


def gather(layers, owner, query_t, key, latent):
    any_space = pl.BlockSpec(memory_space=pl.ANY)
    smem = pl.BlockSpec(memory_space=pltpu.SMEM)
    vmem = pl.BlockSpec(memory_space=pltpu.VMEM)
    return pl.pallas_call(
        gather_kernel,
        out_shape=(pltpu.VMEM((8, 192, COLS), BF16), pltpu.VMEM((8, 64, COLS), BF16), pltpu.VMEM((768, COLS), BF16)),
        in_specs=[smem, smem, any_space, any_space, any_space],
        out_specs=[vmem, vmem, vmem],
        scratch_shapes=[
            pltpu.VMEM((4, QROWS, LAYERS, 4 * COLS), BF16),
            pltpu.VMEM((LAYERS, KROWS, 16 * COLS), BF16),
            pltpu.VMEM((768, 1536), BF16),
            pltpu.VMEM((16, ROWS, COLS), BF16),
            pltpu.VMEM((8, 16, ROWS, COLS), BF16),
            pltpu.VMEM((256, 256), BF16),
            pltpu.VMEM((8, 768, 256), BF16),
            pltpu.VMEM((768, COLS), F32),
            pltpu.SemaphoreType.DMA((6,)),
            pltpu.SemaphoreType.DMA((127,)),
            pltpu.SemaphoreType.DMA((4, 32)),
        ],
        compiler_params=pltpu.CompilerParams(collective_id=0, has_side_effects=True, vmem_limit_bytes=44 << 20),
    )(layers, owner, query_t, key, latent)


def expand_kernel(uq_ref, uk_ref, p_ref, absorbed_ref, projected_ref, mixed):
    step = pl.program_id(0)
    nt = (((1,), (1,)), ((), ()))
    head = pl.ds(pl.multiple_of(step * 128, 128), 128)
    absorbed_ref[0] = lax.dot_general(uq_ref[:, head], uk_ref[:, head], nt, preferred_element_type=F32).astype(BF16)
    rows = pl.ds(pl.multiple_of(step * 96, 32), 96)
    for h in range(8):
        part = lax.dot_general(p_ref[rows, h * 128:(h + 1) * 128], uk_ref[:, h * 128:(h + 1) * 128], nt, preferred_element_type=F32)
        for lane in range(4):
            mixed[lane, pl.ds(h, 96, stride=8), :] = part[:, lane * 128:(lane + 1) * 128]
    for lane in range(4):
        projected_ref[:, :, lane * 128:(lane + 1) * 128] = mixed[lane].reshape(96, 8, 128).astype(BF16)


def expand(uq, uk, p):
    vmem = pl.BlockSpec(memory_space=pltpu.VMEM)
    return pl.pallas_call(
        expand_kernel,
        grid=(8,),
        out_shape=(jax.ShapeDtypeStruct((8, 1536, 512), BF16), jax.ShapeDtypeStruct((768, 8, 512), BF16)),
        in_specs=[vmem, vmem, vmem],
        out_specs=[pl.BlockSpec((1, 1536, 512), lambda i: (i, 0, 0)), pl.BlockSpec((96, 8, 512), lambda i: (i, 0, 0))],
        scratch_shapes=[pltpu.VMEM((4, 768, 128), F32)],
        compiler_params=pltpu.CompilerParams(vmem_limit_bytes=32 << 20),
    )(uq, uk, p)


def shards(changed_layers, bucket_owner, query_up, key_up, query_latent):
    uq, uk, p = gather(changed_layers, bucket_owner, query_up.transpose(1, 0, 2), key_up, query_latent)
    absorbed, projected = expand(uq.reshape(1536, COLS), uk.reshape(512, COLS), p)
    return absorbed[None], projected[None]


def solution(mesh):
    in_specs = (
        P(),
        P(),
        P(None, ("replica", "tp"), None),
        P(None, ("replica", "tp"), None),
        P("replica", None),
    )
    out_specs = (P(None, "tp", None, None), P(None, "replica", "tp", None))
    return jax.shard_map(shards, mesh=mesh, in_specs=in_specs, out_specs=out_specs, check_vma=False)
```

```python
import jax
import jax.numpy as jnp
from jax import lax
from jax.experimental import pallas as pl
from jax.experimental.pallas import tpu as pltpu
from jax.sharding import PartitionSpec as P

MESH = pl.DeviceIdType.MESH
BF16, F32 = jnp.bfloat16, jnp.float32

DX = (0, 1, 3, 2)
QROWS, KROWS, LAYERS = 12, 4, 4
COLS, LANES = 1024, 256
QB, KB = 48, 16
HEADS_HERE, HEAD, KEYS, QUERIES, LATENTS = 8, 128, 512, 1536, 768
SLAB = 192


def place():
    r, t = lax.axis_index("replica"), lax.axis_index("tp")
    return t // 4, (t // 2) % 2, t % 2, r // 4, r % 4


def flip(bit, by):
    return 1 - bit if by else bit


def device(dx=0, e=0, f=0, g=0, dz=0):
    x, y_lo, c, y_hi, z = place()
    return flip(y_hi, g) * 4 + (z + dz) % 4, (((x + dx) % 4) * 2 + flip(y_lo, e)) * 2 + flip(c, f)


def steps(value, size, count):
    return sum((value >= size * k).astype(jnp.int32) for k in range(1, count))


def raw_place(owner_ref, bucket):
    found = jnp.zeros_like(bucket)
    for b in range(16):
        t = owner_ref[b]
        found = jnp.where(bucket == b, ((t // 2) % 2) * 8 + (t // 4) * 2 + t % 2, found)
    return found


def one_hot(wanted, width):
    lane = lax.broadcasted_iota(jnp.int32, (wanted.shape[0], width), 1)
    return jnp.where(lane == wanted, 1.0, 0.0).astype(BF16)


def column(size):
    return lax.broadcasted_iota(jnp.int32, (size, 1), 0)


def query_order(owner_ref):
    out = column(4 * SLAB)
    i = steps(out, SLAB, 4)
    within = out - SLAB * i
    bucket = steps(within, QROWS, 16)
    row = within - QROWS * bucket
    p = steps(row, 4, 3)
    return one_hot(raw_place(owner_ref, bucket) * QB + p * 16 + i * 4 + row - 4 * p, 16 * QB)


def key_order(owner_ref):
    out = column(256)
    i = steps(out, 64, 4)
    within = out - 64 * i
    bucket = steps(within, KROWS, 16)
    return one_hot(raw_place(owner_ref, bucket) * KB + i * 4 + within - KROWS * bucket, 256)


def changed_rows(layer):
    out = column(QB + KB)
    p = steps(out, 16, 4)
    i = steps(out - 16 * p, 4, 4)
    j = out - 16 * p - 4 * i
    row = jnp.where(p < 3, (4 * p + j) * LAYERS + layer, QROWS * LAYERS + layer * KROWS + j)
    return one_hot(i * 64 + row, 256)


def gather_kernel(layer_hbm, owner_hbm, q_hbm, k_hbm, lat_hbm, absorbed_ref, uq_ref, ukt_ref, p_ref,
                  layer_ref, owner_ref, qv, kv, lat, mine, side_k, side_q, held_k, held_q, order_k, order_q, lats, uk, uq, acc,
                  load_sem, send_sem, x_sem, k_sem, q_sem):
    x, y_lo, c, y_hi, z = place()
    y = y_hi * 2 + y_lo
    my_place = x * 2 + c
    barrier = pltpu.get_barrier_semaphore()
    partners = [device(dx=dx, f=f) for dx in DX for f in range(2) if dx or f]
    partners += [device(e=e, f=f, g=g, dz=dz) for e, g, dz in ((1, 0, 0), (0, 1, 0), (1, 1, 0), (0, 0, 1), (0, 0, 3)) for f in range(2)]
    for to in partners:
        pl.semaphore_signal(barrier, inc=1, device_id=to, device_id_type=MESH)

    loads = []
    for n, dx in enumerate(DX):
        columns = pl.ds(pl.multiple_of(((x + dx) % 4) * 4 * COLS, 4 * COLS), 4 * COLS)
        loads.append((pltpu.make_async_copy(q_hbm.at[:, :, columns], qv.at[n], load_sem.at[n]),
                      pltpu.make_async_copy(k_hbm.at[:, :, columns], kv.at[n], load_sem.at[4 + n])))
    load_lat = pltpu.make_async_copy(lat_hbm, lat, load_sem.at[8])
    load_layer = pltpu.make_async_copy(layer_hbm, layer_ref, load_sem.at[9])
    load_owner = pltpu.make_async_copy(owner_hbm, owner_ref, load_sem.at[10])
    load_layer.start()
    for pair in loads:
        for load in pair:
            load.start()
    load_owner.start()
    load_lat.start()
    load_layer.wait()
    pick = changed_rows(layer_ref[0])

    sends = []

    def send(source, target, sem, to):
        copy = pltpu.make_async_remote_copy(src_ref=source, dst_ref=target, send_sem=send_sem.at[len(sends)], recv_sem=sem,
                                            device_id=to, device_id_type=MESH)
        copy.start()
        sends.append(copy)

    def arrive(block, sem):
        pltpu.make_async_remote_copy(src_ref=block, dst_ref=block, send_sem=send_sem.at[0], recv_sem=sem,
                                     device_id=partners[0], device_id_type=MESH).wait_recv()

    def row_at(row, dz):
        return (z + dz) % 4, flip(y_hi, row // 2) * 2 + flip(y_lo, row % 2)

    def keys(row, dz):
        at = row_at(row, dz)
        return held_k.at[at[0], at[1]]

    def queries(row, dz, n):
        at = row_at(row, dz)
        return held_q.at[at[0], at[1], pl.ds(((x + DX[n]) % 4) * 2, 2)]

    def send_keys(row, dz, to, row_there, dz_there):
        send(keys(row, dz), keys(row, dz), k_sem.at[dz_there, row_there], to)

    def send_queries(row, dz, n, to, row_there, dz_there):
        send(queries(row, dz, n), queries(row, dz, n), q_sem.at[dz_there, row_there, n], to)

    up, down = device(dz=1), device(dz=3)
    beside, across, beyond = device(e=1), device(g=1), device(e=1, g=1)

    def keys_along_z(row):
        send_keys(row, 0, up, row, 3)
        send_keys(row, 0, down, row, 1)

    def queries_along_z(row, n):
        send_queries(row, 0, n, up, row, 3)
        send_queries(row, 0, n, down, row, 1)

    def keys_along_y():
        send_keys(0, 0, across, 2, 0)
        for to, row in ((beside, 1), (beyond, 3)):
            send(side_k, keys(0, 0), k_sem.at[0, row], to)

    def queries_along_y(n, e):
        if e == 0:
            send_queries(0, 0, n, across, 2, 0)
            return
        for to, row in ((beside, 1), (beyond, 3)):
            send(side_q.at[pl.ds(((x + DX[n]) % 4) * 2, 2)], queries(0, 0, n), q_sem.at[0, row, n], to)

    def x_index(dx, f):
        return dx * 2 + f

    def arrive_x_keys(n, f):
        at = ((x + DX[n]) % 4) * 2 + flip(c, f)
        arrive(held_k.at[z, y, at], x_sem.at[0, 0, x_index(DX[n], f)])
        arrive(side_k.at[at], x_sem.at[1, 0, x_index(DX[n], f)])

    def arrive_x_queries(n, f, e):
        at = ((x + DX[n]) % 4) * 2 + flip(c, f)
        arrive(side_q.at[at] if e else held_q.at[z, y, at], x_sem.at[e, 1, x_index(DX[n], f)])

    def along_x(n, f, e, part):
        to, there = device(dx=DX[n], f=f), x_index((4 - DX[n]) % 4, f)
        source = mine.at[n * 4 + e * 2 + f]
        if part == 0:
            send(source.at[pl.ds(QB, KB)], side_k.at[my_place] if e else held_k.at[z, y, my_place], x_sem.at[e, 0, there], to)
        else:
            send(source.at[pl.ds(0, QB)], side_q.at[my_place] if e else held_q.at[z, y, my_place], x_sem.at[e, 1, there], to)

    for n, dx in enumerate(DX):
        for load in loads[n]:
            load.wait()
        for e in range(2):
            for f in range(2):
                inner = (flip(y_lo, e) * 2 + flip(c, f)) * COLS
                parts = []
                for i in range(4):
                    columns = pl.ds(pl.multiple_of(inner + i * LANES, LANES), LANES)
                    parts.append(qv[n, :, :, columns].reshape(QROWS * LAYERS, LANES))
                    parts.append(kv[n, :, :, columns].reshape(KROWS * LAYERS, LANES))
                block = jnp.dot(pick, jnp.concatenate(parts, 0), preferred_element_type=F32).astype(BF16)
                mine[n * 4 + e * 2 + f] = block
                if not (dx or f):
                    if e:
                        side_k[my_place] = block[QB:]
                    else:
                        held_q[z, y, my_place] = block[:QB]
                        held_k[z, y, my_place] = block[QB:]
        if n == 0:
            pl.semaphore_wait(barrier, len(partners))
            own = held_q.at[z, y, my_place]
            for f in range(2):
                block = mine.at[f, pl.ds(0, QB)]
                send(block, own, q_sem.at[3, 0, 0], device(dz=1, f=f))
                send(block, own, q_sem.at[1, 0, 0], device(dz=3, f=f))
                send(block, own, q_sem.at[0, 2, 0], device(g=1, f=f))
                block = mine.at[2 + f, pl.ds(0, QB)]
                send(block, own, q_sem.at[0, 1, 0], device(e=1, f=f))
                send(block, own, q_sem.at[0, 3, 0], device(e=1, g=1, f=f))
    for n in range(4):
        for f in range(2):
            if DX[n] or f:
                for e in range(2):
                    along_x(n, f, e, 0)
    for e in range(2):
        for n in (1, 2):
            for f in range(2):
                along_x(n, f, e, 1)
    for e in range(2):
        for f in range(2):
            along_x(3, f, e, 1)
    along_x(0, 1, 0, 1)

    def row_zero(n, e):
        for f in range(2):
            arrive_x_queries(n, f, e)
        if e == 0:
            queries_along_z(0, n)
        queries_along_y(n, e)

    def row_on(row, n):
        arrive(queries(row, 0, n), q_sem.at[0, row, n])
        queries_along_z(row, n)

    def onward(row, n):
        dz, to = ((3, up), (1, down))[row]
        arrive(queries(row, dz, n), q_sem.at[dz, row, n])
        send_queries(row, dz, n, to, row, 2)

    def keys_onward(row):
        dz, to = ((3, up), (1, down))[row]
        arrive(keys(row, dz), k_sem.at[dz, row])
        send_keys(row, dz, to, row, 2)

    def slab_index(g, dz):
        return flip(y_hi, g) * 4 + (z + dz) % 4

    def query_slab(g, dz, first=False, last=False, spare=None):
        at_y = flip(y_hi, g) * 2
        r = slab_index(g, dz)
        raw = held_q[(z + dz) % 4, pl.ds(at_y, 2)].reshape(16 * QB, LANES)
        ordered = jnp.dot(order_q[...], raw, preferred_element_type=F32).astype(BF16)
        for i in range(4):
            uq[r, :, i * LANES:(i + 1) * LANES] = ordered[i * SLAB:(i + 1) * SLAB]
        if spare is not None:
            uq_ref[spare] = uq[r]
        term = jnp.dot(lats[r], uq[r], preferred_element_type=F32)
        total = term if first else acc[...] + term
        if last:
            p_ref[...] = total.astype(BF16)
        else:
            acc[...] = total

    def absorb(g, dz):
        r = slab_index(g, dz)
        rows = pl.ds(pl.multiple_of(r * SLAB, 64), SLAB)
        for h in range(HEADS_HERE):
            absorbed_ref[h, rows] = jnp.dot(uq[r, :, h * HEAD:(h + 1) * HEAD], ukt_ref[h], preferred_element_type=F32).astype(BF16)

    def hand_across(row):
        for n in range(4):
            arrive(queries(row, 2, n), q_sem.at[2, row, n])
            send_queries(row, 2, n, across, row + 2, 2)

    load_owner.wait()
    order_k[...] = key_order(owner_ref)
    order_q[...] = query_order(owner_ref)
    load_lat.wait()
    for r in range(8):
        lats[r] = lat[:, r * SLAB:(r + 1) * SLAB]

    for n in range(4):
        for f in range(2):
            if DX[n] or f:
                arrive_x_keys(n, f)
    keys_along_z(0)
    keys_along_y()
    for e in range(2):
        row_zero(1, e)
        row_zero(2, e)
    row_zero(3, 0)
    row_zero(3, 1)
    for row in (1, 3, 2):
        arrive(keys(row, 0), k_sem.at[0, row])
        keys_along_z(row)
    keys_onward(0)
    keys_onward(1)
    for n in range(4):
        row_on(1, n)
    for n in range(4):
        onward(0, n)
    for row in (0, 1):
        arrive(keys(row, 2), k_sem.at[2, row])
        send_keys(row, 2, across, row + 2, 2)
    for n in range(4):
        onward(1, n)
    arrive_x_queries(0, 1, 0)
    query_slab(0, 0, first=True)
    for n in range(4):
        row_on(3, n)
    hand_across(0)
    for n in range(4):
        row_on(2, n)
    hand_across(1)
    query_slab(1, 0)
    for dz in (1, 3):
        row = 0 if dz == 1 else 1
        for n in range(4):
            arrive(queries(row, dz, n), q_sem.at[dz, row, n])
        query_slab(0, dz)
    for dz in (1, 3):
        for row in range(4):
            if (row, dz) not in ((0, 3), (1, 1)):
                arrive(keys(row, dz), k_sem.at[dz, row])
    for row in (2, 3):
        arrive(keys(row, 2), k_sem.at[2, row])
    for at_z in range(4):
        for at_y in range(2):
            raw = held_k[at_z, 2 * at_y:2 * at_y + 2].reshape(256, LANES)
            ordered = jnp.dot(order_k[...], raw, preferred_element_type=F32).astype(BF16)
            for i in range(4):
                uk[(at_y * 4 + at_z) * 64:(at_y * 4 + at_z) * 64 + 64, i * LANES:(i + 1) * LANES] = ordered[i * 64:(i + 1) * 64]
    for h in range(HEADS_HERE):
        ukt_ref[h] = uk[:, h * HEAD:(h + 1) * HEAD].T
    for g, dz in ((0, 0), (1, 0), (0, 1), (0, 3)):
        absorb(g, dz)
    query_slab(0, 2)
    absorb(0, 2)
    for row in (2, 3):
        for n in range(4):
            arrive(queries(row, 2, n), q_sem.at[2, row, n])
    query_slab(1, 2)
    absorb(1, 2)
    for dz in (1, 3):
        for row in (2, 3):
            for n in range(4):
                arrive(queries(row, dz, n), q_sem.at[dz, row, n])
        query_slab(1, dz, last=dz == 3, spare=dz // 2)
    for copy in sends:
        copy.wait_send()


def gather(layers, owner, query_t, key, latent):
    any_space = pl.BlockSpec(memory_space=pl.ANY)
    vmem = pl.BlockSpec(memory_space=pltpu.VMEM)
    return pl.pallas_call(
        gather_kernel,
        out_shape=(pltpu.VMEM((HEADS_HERE, QUERIES, KEYS), BF16), pltpu.VMEM((2, SLAB, COLS), BF16),
                   pltpu.VMEM((HEADS_HERE, HEAD, KEYS), BF16), pltpu.VMEM((LATENTS, COLS), BF16)),
        in_specs=[any_space] * 5,
        out_specs=[vmem] * 4,
        scratch_shapes=[
            pltpu.SMEM((4,), jnp.int32),
            pltpu.SMEM((16,), jnp.int32),
            pltpu.VMEM((4, QROWS, LAYERS, 4 * COLS), BF16),
            pltpu.VMEM((4, LAYERS, KROWS, 4 * COLS), BF16),
            pltpu.VMEM((LATENTS, QUERIES), BF16),
            pltpu.VMEM((16, QB + KB, LANES), BF16),
            pltpu.VMEM((8, KB, LANES), BF16),
            pltpu.VMEM((8, QB, LANES), BF16),
            pltpu.VMEM((4, 4, 8, KB, LANES), BF16),
            pltpu.VMEM((4, 4, 8, QB, LANES), BF16),
            pltpu.VMEM((256, 256), BF16),
            pltpu.VMEM((4 * SLAB, 16 * QB), BF16),
            pltpu.VMEM((8, LATENTS, SLAB), BF16),
            pltpu.VMEM((KEYS, COLS), BF16),
            pltpu.VMEM((8, SLAB, COLS), BF16),
            pltpu.VMEM((LATENTS, COLS), F32),
            pltpu.SemaphoreType.DMA((11,)),
            pltpu.SemaphoreType.DMA((107,)),
            pltpu.SemaphoreType.DMA((2, 2, 8)),
            pltpu.SemaphoreType.DMA((4, 4)),
            pltpu.SemaphoreType.DMA((4, 4, 4)),
        ],
        compiler_params=pltpu.CompilerParams(collective_id=0, has_side_effects=True, vmem_limit_bytes=43 << 20),
    )(layers, owner, query_t, key, latent)


CHUNK = 192


def expand_kernel(done_ref, uq_ref, ukt_ref, p_ref, absorbed_hbm, projected_hbm, rest, mixed, projected, out_sem, rest_sem, p_sem):
    _, _, _, y_hi, z = place()

    def rows(g, dz):
        return pl.ds(pl.multiple_of((flip(y_hi, g) * 4 + (z + dz) % 4) * SLAB, 64), SLAB)

    copies = []
    for n, (g, dz) in enumerate(((0, 0), (1, 0), (0, 1), (0, 3), (0, 2), (1, 2))):
        copies.append(pltpu.make_async_copy(done_ref.at[:, rows(g, dz)], absorbed_hbm.at[:, rows(g, dz)], out_sem.at[n]))
        copies[-1].start()
    for n in range(LATENTS // CHUNK):
        for h in range(HEADS_HERE):
            part = jnp.dot(p_ref[n * CHUNK:(n + 1) * CHUNK, h * HEAD:(h + 1) * HEAD], ukt_ref[h], preferred_element_type=F32)
            for lane in range(4):
                mixed[lane, pl.ds(h, CHUNK, stride=8), :] = part[:, lane * 128:(lane + 1) * 128]
        for lane in range(4):
            projected[n, :, :, lane * 128:(lane + 1) * 128] = mixed[lane].reshape(CHUNK, 8, 128).astype(BF16)
        copies.append(pltpu.make_async_copy(projected.at[n], projected_hbm.at[pl.ds(n * CHUNK, CHUNK)], p_sem.at[n]))
        copies[-1].start()
        if n < 2:
            for h in range(HEADS_HERE):
                rest[n, h] = jnp.dot(uq_ref[n, :, h * HEAD:(h + 1) * HEAD], ukt_ref[h], preferred_element_type=F32).astype(BF16)
            copies.append(pltpu.make_async_copy(rest.at[n], absorbed_hbm.at[:, rows(1, 1 + 2 * n)], rest_sem.at[n]))
            copies[-1].start()
    for copy in copies:
        copy.wait()


def expand(done, uq, ukt, p):
    vmem = pl.BlockSpec(memory_space=pltpu.VMEM)
    return pl.pallas_call(
        expand_kernel,
        out_shape=(jax.ShapeDtypeStruct((HEADS_HERE, QUERIES, KEYS), BF16), jax.ShapeDtypeStruct((LATENTS, HEADS_HERE, KEYS), BF16)),
        in_specs=[vmem] * 4,
        out_specs=[pl.BlockSpec(memory_space=pl.ANY)] * 2,
        scratch_shapes=[
            pltpu.VMEM((2, HEADS_HERE, SLAB, KEYS), BF16),
            pltpu.VMEM((4, CHUNK * 8, 128), F32),
            pltpu.VMEM((LATENTS // CHUNK, CHUNK, HEADS_HERE, KEYS), BF16),
            pltpu.SemaphoreType.DMA((6,)),
            pltpu.SemaphoreType.DMA((2,)),
            pltpu.SemaphoreType.DMA((LATENTS // CHUNK,)),
        ],
        compiler_params=pltpu.CompilerParams(vmem_limit_bytes=24 << 20),
    )(done, uq, ukt, p)


def shards(changed_layers, bucket_owner, query_up, key_up, query_latent):
    done, uq, ukt, p = gather(changed_layers, bucket_owner, query_up.transpose(1, 0, 2), key_up, query_latent)
    absorbed, projected = expand(done, uq, ukt, p)
    return absorbed[None], projected[None]


def solution(mesh):
    in_specs = (
        P(),
        P(),
        P(None, ("replica", "tp"), None),
        P(None, ("replica", "tp"), None),
        P("replica", None),
    )
    out_specs = (P(None, "tp", None, None), P(None, "replica", "tp", None))
    return jax.shard_map(shards, mesh=mesh, in_specs=in_specs, out_specs=out_specs, check_vma=False)
```

```python
import jax
import jax.numpy as jnp
from jax import lax
from jax.experimental import pallas as pl
from jax.experimental.pallas import tpu as pltpu
from jax.sharding import PartitionSpec as P

MESH = pl.DeviceIdType.MESH
BF16, F32 = jnp.bfloat16, jnp.float32

DX = (0, 1, 3, 2)
QROWS, KROWS, LAYERS = 12, 4, 4
COLS, LANES = 1024, 256
QB, KB = 48, 16
HEADS_HERE, HEAD, KEYS, QUERIES, LATENTS = 8, 128, 512, 1536, 768
SLAB = 192


def place():
    r, t = lax.axis_index("replica"), lax.axis_index("tp")
    return t // 4, (t // 2) % 2, t % 2, r // 4, r % 4


def flip(bit, by):
    return 1 - bit if by else bit


def device(dx=0, e=0, f=0, g=0, dz=0):
    x, y_lo, c, y_hi, z = place()
    return flip(y_hi, g) * 4 + (z + dz) % 4, (((x + dx) % 4) * 2 + flip(y_lo, e)) * 2 + flip(c, f)


def steps(value, size, count):
    return sum((value >= size * k).astype(jnp.int32) for k in range(1, count))


def raw_place(owner_ref, bucket):
    found = jnp.zeros_like(bucket)
    for b in range(16):
        t = owner_ref[b]
        found = jnp.where(bucket == b, ((t // 2) % 2) * 8 + (t // 4) * 2 + t % 2, found)
    return found


def one_hot(wanted, width):
    lane = lax.broadcasted_iota(jnp.int32, (wanted.shape[0], width), 1)
    return jnp.where(lane == wanted, 1.0, 0.0).astype(BF16)


def column(size):
    return lax.broadcasted_iota(jnp.int32, (size, 1), 0)


def query_order(owner_ref):
    out = column(4 * SLAB)
    i = steps(out, SLAB, 4)
    within = out - SLAB * i
    bucket = steps(within, QROWS, 16)
    row = within - QROWS * bucket
    p = steps(row, 4, 3)
    return one_hot(raw_place(owner_ref, bucket) * QB + p * 16 + i * 4 + row - 4 * p, 16 * QB)


def key_order(owner_ref):
    out = column(256)
    i = steps(out, 64, 4)
    within = out - 64 * i
    bucket = steps(within, KROWS, 16)
    return one_hot(raw_place(owner_ref, bucket) * KB + i * 4 + within - KROWS * bucket, 256)


def changed_rows(layer):
    out = column(QB + KB)
    p = steps(out, 16, 4)
    i = steps(out - 16 * p, 4, 4)
    j = out - 16 * p - 4 * i
    row = jnp.where(p < 3, (4 * p + j) * LAYERS + layer, QROWS * LAYERS + layer * KROWS + j)
    return one_hot(i * 64 + row, 256)


def gather_kernel(layer_hbm, owner_hbm, q_hbm, k_hbm, lat_hbm, absorbed_ref, uq_ref, ukt_ref, p_ref,
                  layer_ref, owner_ref, qv, kv, lat, mine, side_k, side_q, held_k, held_q, order_k, order_q, lats, uk, uq, acc,
                  load_sem, send_sem, x_sem, k_sem, q_sem):
    x, y_lo, c, y_hi, z = place()
    y = y_hi * 2 + y_lo
    my_place = x * 2 + c
    barrier = pltpu.get_barrier_semaphore()
    partners = [device(dx=dx, f=f) for dx in DX for f in range(2) if dx or f]
    partners += [device(e=e, f=f, g=g, dz=dz) for e, g, dz in ((1, 0, 0), (0, 1, 0), (1, 1, 0), (0, 0, 1), (0, 0, 3)) for f in range(2)]
    for to in partners:
        pl.semaphore_signal(barrier, inc=1, device_id=to, device_id_type=MESH)

    loads = []
    for n, dx in enumerate(DX):
        columns = pl.ds(pl.multiple_of(((x + dx) % 4) * 4 * COLS, 4 * COLS), 4 * COLS)
        loads.append((pltpu.make_async_copy(q_hbm.at[:, :, columns], qv.at[n], load_sem.at[n]),
                      pltpu.make_async_copy(k_hbm.at[:, :, columns], kv.at[n], load_sem.at[4 + n])))
    load_lat = pltpu.make_async_copy(lat_hbm, lat, load_sem.at[8])
    load_layer = pltpu.make_async_copy(layer_hbm, layer_ref, load_sem.at[9])
    load_owner = pltpu.make_async_copy(owner_hbm, owner_ref, load_sem.at[10])
    load_layer.start()
    for pair in loads:
        for load in pair:
            load.start()
    load_owner.start()
    load_lat.start()
    load_layer.wait()
    pick = changed_rows(layer_ref[0])

    sends = []

    def send(source, target, sem, to):
        copy = pltpu.make_async_remote_copy(src_ref=source, dst_ref=target, send_sem=send_sem.at[len(sends)], recv_sem=sem,
                                            device_id=to, device_id_type=MESH)
        copy.start()
        sends.append(copy)

    def arrive(block, sem):
        pltpu.make_async_remote_copy(src_ref=block, dst_ref=block, send_sem=send_sem.at[0], recv_sem=sem,
                                     device_id=partners[0], device_id_type=MESH).wait_recv()

    def row_at(row, dz):
        return (z + dz) % 4, flip(y_hi, row // 2) * 2 + flip(y_lo, row % 2)

    def keys(row, dz):
        at = row_at(row, dz)
        return held_k.at[at[0], at[1]]

    def queries(row, dz, n):
        at = row_at(row, dz)
        return held_q.at[at[0], at[1], pl.ds(((x + DX[n]) % 4) * 2, 2)]

    def send_keys(row, dz, to, row_there, dz_there):
        send(keys(row, dz), keys(row, dz), k_sem.at[dz_there, row_there], to)

    def send_queries(row, dz, n, to, row_there, dz_there):
        send(queries(row, dz, n), queries(row, dz, n), q_sem.at[dz_there, row_there, n], to)

    up, down = device(dz=1), device(dz=3)
    beside, across, beyond = device(e=1), device(g=1), device(e=1, g=1)

    def keys_along_z(row):
        send_keys(row, 0, up, row, 3)
        send_keys(row, 0, down, row, 1)

    def queries_along_z(row, n):
        send_queries(row, 0, n, up, row, 3)
        send_queries(row, 0, n, down, row, 1)

    def keys_along_y():
        send_keys(0, 0, across, 2, 0)
        for to, row in ((beside, 1), (beyond, 3)):
            send(side_k, keys(0, 0), k_sem.at[0, row], to)

    def queries_along_y(n, e):
        if e == 0:
            send_queries(0, 0, n, across, 2, 0)
            return
        for to, row in ((beside, 1), (beyond, 3)):
            send(side_q.at[pl.ds(((x + DX[n]) % 4) * 2, 2)], queries(0, 0, n), q_sem.at[0, row, n], to)

    def x_index(dx, f):
        return dx * 2 + f

    def arrive_x_keys(n, f):
        at = ((x + DX[n]) % 4) * 2 + flip(c, f)
        arrive(held_k.at[z, y, at], x_sem.at[0, 0, x_index(DX[n], f)])
        arrive(side_k.at[at], x_sem.at[1, 0, x_index(DX[n], f)])

    def arrive_x_queries(n, f, e):
        at = ((x + DX[n]) % 4) * 2 + flip(c, f)
        arrive(side_q.at[at] if e else held_q.at[z, y, at], x_sem.at[e, 1, x_index(DX[n], f)])

    def along_x(n, f, e, part):
        to, there = device(dx=DX[n], f=f), x_index((4 - DX[n]) % 4, f)
        source = mine.at[n * 4 + e * 2 + f]
        if part == 0:
            send(source.at[pl.ds(QB, KB)], side_k.at[my_place] if e else held_k.at[z, y, my_place], x_sem.at[e, 0, there], to)
        else:
            send(source.at[pl.ds(0, QB)], side_q.at[my_place] if e else held_q.at[z, y, my_place], x_sem.at[e, 1, there], to)

    for n, dx in enumerate(DX):
        for load in loads[n]:
            load.wait()
        for e in range(2):
            for f in range(2):
                inner = (flip(y_lo, e) * 2 + flip(c, f)) * COLS
                parts = []
                for i in range(4):
                    columns = pl.ds(pl.multiple_of(inner + i * LANES, LANES), LANES)
                    parts.append(qv[n, :, :, columns].reshape(QROWS * LAYERS, LANES))
                    parts.append(kv[n, :, :, columns].reshape(KROWS * LAYERS, LANES))
                block = jnp.dot(pick, jnp.concatenate(parts, 0), preferred_element_type=F32).astype(BF16)
                mine[n * 4 + e * 2 + f] = block
                if not (dx or f):
                    if e:
                        side_k[my_place] = block[QB:]
                    else:
                        held_q[z, y, my_place] = block[:QB]
                        held_k[z, y, my_place] = block[QB:]
        if n == 0:
            pl.semaphore_wait(barrier, len(partners))
            own = held_q.at[z, y, my_place]
            for f in range(2):
                block = mine.at[f, pl.ds(0, QB)]
                send(block, own, q_sem.at[3, 0, 0], device(dz=1, f=f))
                send(block, own, q_sem.at[1, 0, 0], device(dz=3, f=f))
                send(block, own, q_sem.at[0, 2, 0], device(g=1, f=f))
                block = mine.at[2 + f, pl.ds(0, QB)]
                send(block, own, q_sem.at[0, 1, 0], device(e=1, f=f))
                send(block, own, q_sem.at[0, 3, 0], device(e=1, g=1, f=f))
    for n in range(4):
        for f in range(2):
            if DX[n] or f:
                for e in range(2):
                    along_x(n, f, e, 0)
    for e in range(2):
        for n in (1, 2):
            for f in range(2):
                along_x(n, f, e, 1)
    for e in range(2):
        for f in range(2):
            along_x(3, f, e, 1)
    along_x(0, 1, 0, 1)

    def row_zero(n, e):
        for f in range(2):
            arrive_x_queries(n, f, e)
        if e == 0:
            queries_along_z(0, n)
        queries_along_y(n, e)

    def row_on(row, n):
        arrive(queries(row, 0, n), q_sem.at[0, row, n])
        queries_along_z(row, n)

    def onward(row, n):
        dz, to = ((3, up), (1, down))[row]
        arrive(queries(row, dz, n), q_sem.at[dz, row, n])
        send_queries(row, dz, n, to, row, 2)

    def keys_onward(row):
        dz, to = ((3, up), (1, down))[row]
        arrive(keys(row, dz), k_sem.at[dz, row])
        send_keys(row, dz, to, row, 2)

    def slab_index(g, dz):
        return flip(y_hi, g) * 4 + (z + dz) % 4

    def query_slab(g, dz, first=False, last=False, spare=None):
        at_y = flip(y_hi, g) * 2
        r = slab_index(g, dz)
        raw = held_q[(z + dz) % 4, pl.ds(at_y, 2)].reshape(16 * QB, LANES)
        ordered = jnp.dot(order_q[...], raw, preferred_element_type=F32).astype(BF16)
        for i in range(4):
            uq[r, :, i * LANES:(i + 1) * LANES] = ordered[i * SLAB:(i + 1) * SLAB]
        if spare is not None:
            uq_ref[spare] = uq[r]
        term = jnp.dot(lats[r], uq[r], preferred_element_type=F32)
        total = term if first else acc[...] + term
        if last:
            p_ref[...] = total.astype(BF16)
        else:
            acc[...] = total

    def absorb(g, dz):
        r = slab_index(g, dz)
        rows = pl.ds(pl.multiple_of(r * SLAB, 64), SLAB)
        for h in range(HEADS_HERE):
            absorbed_ref[h, rows] = jnp.dot(uq[r, :, h * HEAD:(h + 1) * HEAD], ukt_ref[h], preferred_element_type=F32).astype(BF16)

    def hand_across(row):
        for n in range(4):
            arrive(queries(row, 2, n), q_sem.at[2, row, n])
            send_queries(row, 2, n, across, row + 2, 2)

    load_owner.wait()
    order_k[...] = key_order(owner_ref)
    order_q[...] = query_order(owner_ref)
    load_lat.wait()
    for r in range(8):
        lats[r] = lat[:, r * SLAB:(r + 1) * SLAB]

    for n in range(4):
        for f in range(2):
            if DX[n] or f:
                arrive_x_keys(n, f)
    keys_along_z(0)
    keys_along_y()
    for e in range(2):
        row_zero(1, e)
        row_zero(2, e)
    row_zero(3, 0)
    row_zero(3, 1)
    for row in (1, 3, 2):
        arrive(keys(row, 0), k_sem.at[0, row])
        keys_along_z(row)
    keys_onward(0)
    keys_onward(1)
    for n in range(4):
        row_on(1, n)
    for n in range(4):
        onward(0, n)
    for row in (0, 1):
        arrive(keys(row, 2), k_sem.at[2, row])
        send_keys(row, 2, across, row + 2, 2)
    for n in range(4):
        onward(1, n)
    arrive_x_queries(0, 1, 0)
    query_slab(0, 0, first=True)
    for n in range(4):
        row_on(3, n)
    for n in range(4):
        arrive(queries(0, 1, n), q_sem.at[1, 0, n])
    query_slab(0, 1)
    hand_across(0)
    for n in range(4):
        row_on(2, n)
    hand_across(1)
    query_slab(1, 0)
    for n in range(4):
        arrive(queries(1, 3, n), q_sem.at[3, 1, n])
    query_slab(0, 3)
    for dz in (1, 3):
        for row in range(4):
            if (row, dz) not in ((0, 3), (1, 1)):
                arrive(keys(row, dz), k_sem.at[dz, row])
    for row in (2, 3):
        arrive(keys(row, 2), k_sem.at[2, row])
    for at_z in range(4):
        for at_y in range(2):
            raw = held_k[at_z, 2 * at_y:2 * at_y + 2].reshape(256, LANES)
            ordered = jnp.dot(order_k[...], raw, preferred_element_type=F32).astype(BF16)
            for i in range(4):
                uk[(at_y * 4 + at_z) * 64:(at_y * 4 + at_z) * 64 + 64, i * LANES:(i + 1) * LANES] = ordered[i * 64:(i + 1) * 64]
    for h in range(HEADS_HERE):
        ukt_ref[h] = uk[:, h * HEAD:(h + 1) * HEAD].T
    for g, dz in ((0, 0), (1, 0), (0, 1), (0, 3)):
        absorb(g, dz)
    query_slab(0, 2)
    absorb(0, 2)
    for row in (2, 3):
        for n in range(4):
            arrive(queries(row, 2, n), q_sem.at[2, row, n])
    query_slab(1, 2)
    absorb(1, 2)
    for dz in (1, 3):
        for row in (2, 3):
            for n in range(4):
                arrive(queries(row, dz, n), q_sem.at[dz, row, n])
        query_slab(1, dz, last=dz == 3, spare=dz // 2)
    for copy in sends:
        copy.wait_send()


def gather(layers, owner, query_t, key, latent):
    any_space = pl.BlockSpec(memory_space=pl.ANY)
    vmem = pl.BlockSpec(memory_space=pltpu.VMEM)
    return pl.pallas_call(
        gather_kernel,
        out_shape=(pltpu.VMEM((HEADS_HERE, QUERIES, KEYS), BF16), pltpu.VMEM((2, SLAB, COLS), BF16),
                   pltpu.VMEM((HEADS_HERE, HEAD, KEYS), BF16), pltpu.VMEM((LATENTS, COLS), BF16)),
        in_specs=[any_space] * 5,
        out_specs=[vmem] * 4,
        scratch_shapes=[
            pltpu.SMEM((4,), jnp.int32),
            pltpu.SMEM((16,), jnp.int32),
            pltpu.VMEM((4, QROWS, LAYERS, 4 * COLS), BF16),
            pltpu.VMEM((4, LAYERS, KROWS, 4 * COLS), BF16),
            pltpu.VMEM((LATENTS, QUERIES), BF16),
            pltpu.VMEM((16, QB + KB, LANES), BF16),
            pltpu.VMEM((8, KB, LANES), BF16),
            pltpu.VMEM((8, QB, LANES), BF16),
            pltpu.VMEM((4, 4, 8, KB, LANES), BF16),
            pltpu.VMEM((4, 4, 8, QB, LANES), BF16),
            pltpu.VMEM((256, 256), BF16),
            pltpu.VMEM((4 * SLAB, 16 * QB), BF16),
            pltpu.VMEM((8, LATENTS, SLAB), BF16),
            pltpu.VMEM((KEYS, COLS), BF16),
            pltpu.VMEM((8, SLAB, COLS), BF16),
            pltpu.VMEM((LATENTS, COLS), F32),
            pltpu.SemaphoreType.DMA((11,)),
            pltpu.SemaphoreType.DMA((107,)),
            pltpu.SemaphoreType.DMA((2, 2, 8)),
            pltpu.SemaphoreType.DMA((4, 4)),
            pltpu.SemaphoreType.DMA((4, 4, 4)),
        ],
        compiler_params=pltpu.CompilerParams(collective_id=0, has_side_effects=True, vmem_limit_bytes=43 << 20),
    )(layers, owner, query_t, key, latent)


CHUNK = 192


def expand_kernel(done_ref, uq_ref, ukt_ref, p_ref, absorbed_hbm, projected_hbm, rest, mixed, projected, out_sem, rest_sem, p_sem):
    _, _, _, y_hi, z = place()

    def rows(g, dz):
        return pl.ds(pl.multiple_of((flip(y_hi, g) * 4 + (z + dz) % 4) * SLAB, 64), SLAB)

    copies = []
    for n, (g, dz) in enumerate(((0, 0), (1, 0), (0, 1), (0, 3), (0, 2), (1, 2))):
        copies.append(pltpu.make_async_copy(done_ref.at[:, rows(g, dz)], absorbed_hbm.at[:, rows(g, dz)], out_sem.at[n]))
        copies[-1].start()
    for n in range(LATENTS // CHUNK):
        for h in range(HEADS_HERE):
            part = jnp.dot(p_ref[n * CHUNK:(n + 1) * CHUNK, h * HEAD:(h + 1) * HEAD], ukt_ref[h], preferred_element_type=F32)
            for lane in range(4):
                mixed[lane, pl.ds(h, CHUNK, stride=8), :] = part[:, lane * 128:(lane + 1) * 128]
        for lane in range(4):
            projected[n, :, :, lane * 128:(lane + 1) * 128] = mixed[lane].reshape(CHUNK, 8, 128).astype(BF16)
        copies.append(pltpu.make_async_copy(projected.at[n], projected_hbm.at[pl.ds(n * CHUNK, CHUNK)], p_sem.at[n]))
        copies[-1].start()
        if n < 2:
            for h in range(HEADS_HERE):
                rest[n, h] = jnp.dot(uq_ref[n, :, h * HEAD:(h + 1) * HEAD], ukt_ref[h], preferred_element_type=F32).astype(BF16)
            copies.append(pltpu.make_async_copy(rest.at[n], absorbed_hbm.at[:, rows(1, 1 + 2 * n)], rest_sem.at[n]))
            copies[-1].start()
    for copy in copies:
        copy.wait()


def expand(done, uq, ukt, p):
    vmem = pl.BlockSpec(memory_space=pltpu.VMEM)
    return pl.pallas_call(
        expand_kernel,
        out_shape=(jax.ShapeDtypeStruct((HEADS_HERE, QUERIES, KEYS), BF16), jax.ShapeDtypeStruct((LATENTS, HEADS_HERE, KEYS), BF16)),
        in_specs=[vmem] * 4,
        out_specs=[pl.BlockSpec(memory_space=pl.ANY)] * 2,
        scratch_shapes=[
            pltpu.VMEM((2, HEADS_HERE, SLAB, KEYS), BF16),
            pltpu.VMEM((4, CHUNK * 8, 128), F32),
            pltpu.VMEM((LATENTS // CHUNK, CHUNK, HEADS_HERE, KEYS), BF16),
            pltpu.SemaphoreType.DMA((6,)),
            pltpu.SemaphoreType.DMA((2,)),
            pltpu.SemaphoreType.DMA((LATENTS // CHUNK,)),
        ],
        compiler_params=pltpu.CompilerParams(vmem_limit_bytes=24 << 20),
    )(done, uq, ukt, p)


def shards(changed_layers, bucket_owner, query_up, key_up, query_latent):
    done, uq, ukt, p = gather(changed_layers, bucket_owner, query_up.transpose(1, 0, 2), key_up, query_latent)
    absorbed, projected = expand(done, uq, ukt, p)
    return absorbed[None], projected[None]


def solution(mesh):
    in_specs = (
        P(),
        P(),
        P(None, ("replica", "tp"), None),
        P(None, ("replica", "tp"), None),
        P("replica", None),
    )
    out_specs = (P(None, "tp", None, None), P(None, "replica", "tp", None))
    return jax.shard_map(shards, mesh=mesh, in_specs=in_specs, out_specs=out_specs, check_vma=False)
```
